512 devices in a mesh: dp: 64 (over x, y_hi, z), expert: 4 (over y_lo), tensor: 2 (over core).
Axes of the slice: x: 4, y: 8 (y_hi: 2, y_lo: 4; y = y_hi * 4 + y_lo), z: 8, core: 2. Of those that a mesh axis runs over, the one named last changes fastest.
Arguments:
- saved_rows: bfloat16 [64, 4, 512, 6144], P('dp', 'expert', None, 'tensor'), may hold values from -6 to 6
- grad_hidden: bfloat16 [64, 4, 128, 512], P('dp', 'expert', 'tensor'), may hold values from -0.15625 to 0.15625
- counts: int32 [64, 8], P('dp', 'expert'), may hold values from 1 to 256, as said below
- offsets: int32 [64, 8], P('dp', 'expert'), may hold values from 0 to 256, as said below
- master: float32 [8, 2, 64, 6144], P('expert', 'tensor', 'dp'), may hold values from -1.2 to 1.2
- moment1: float32 [8, 2, 64, 6144], P('expert', 'tensor', 'dp'), may hold values from -3 to 3
- moment2: float32 [8, 2, 64, 6144], P('expert', 'tensor', 'dp'), may hold values from 0.25 to 4
- next_rows: bfloat16 [64, 8, 64, 6144], P('dp', 'expert', None, 'tensor'), may hold values from -6 to 6
Outputs:
- new_master: float32 [8, 2, 64, 6144], P('expert', 'tensor', 'dp')
- new_moment1: float32 [8, 2, 64, 6144], P('expert', 'tensor', 'dp')
- new_moment2: float32 [8, 2, 64, 6144], P('expert', 'tensor', 'dp')
- next_gate: float32 [64, 8, 128, 64], P('dp', 'expert', 'tensor')
The draws below stay inside these ranges and needn't reach their ends.
Inputs may be any that keep to these rules, and one draw needn't show every extreme that they name: `counts`: on every index of dp some expert has exactly 256 rows. On each buffer the experts' rows do not intersect, the first expert's before the second's, and offsets + 256 <= 512; in every draw some buffer's second expert begins at row 256.
All inputs are finite; a program needn't handle non-finite values.
Results may differ from the reference program's by a relative error of at most 0.0029.
Values may be sent and summed in bfloat16 or wider, within the bound.
No kernel may reach another device: no remote copies, remote signals or barrier semaphores. Data moves between devices by JAX's collectives and lax.ppermute only.
A program may use at most 64 MiB of HBM per device.

```python
import math
import jax
import jax.numpy as jnp

D = 6144
EXP_DEV = 2
EXPERTS = 8
BUCKET = 64
HID = 128
ROWS = 512
CAP = 256
NEXT = 64
N_DP = 64
N_EXPERT = 4
N_TENSOR = 2


def layout(key):
    keys = jax.random.split(key, 6)
    level = jax.random.randint(keys[0], (1, EXPERTS), 1, 5)
    raw = jax.random.randint(keys[1], (N_DP, EXPERTS), 0, CAP)
    sizes = 1 + raw * level // 4
    hottest = jax.random.randint(keys[2], (N_DP,), 0, EXPERTS)
    sizes = jnp.where(jnp.arange(EXPERTS)[None, :] == hottest[:, None], CAP, sizes)
    sizes = jnp.minimum(sizes, CAP).astype(jnp.int32)
    paired = sizes.reshape(N_DP, N_EXPERT, 2)
    first_size = paired[:, :, 0]
    forced = (jnp.arange(N_DP * N_EXPERT) == jax.random.randint(keys[3], (), 0, N_DP * N_EXPERT)).reshape(N_DP, N_EXPERT)
    first_start = jax.random.randint(keys[4], (N_DP, N_EXPERT), 0, CAP - first_size + 1)
    first_start = jnp.where(forced, 0, first_start)
    spare = CAP - first_start - first_size
    second_gap = jax.random.randint(keys[5], (N_DP, N_EXPERT), 0, spare + 1)
    second_gap = jnp.where(forced, spare, second_gap)
    second_start = first_start + first_size + second_gap
    starts = jnp.stack([first_start, second_start], axis=2).reshape(N_DP, EXPERTS).astype(jnp.int32)
    return (sizes, starts)


def draw_counts(key, part):
    sizes, starts = layout(key)
    return sizes


def draw_offsets(key, part):
    sizes, starts = layout(key)
    return starts


def spiked(drawn, own_key, source, target, shards_of, factor):
    owner, partner = [(jnp.arange(drawn.shape[position]) // (drawn.shape[position] // shards_of)).reshape([-1 if axis == position else 1 for axis in range(drawn.ndim)]) for position in (source, target)]
    chosen = jax.random.permutation(own_key, shards_of)[partner]
    strong = (owner == chosen) | (owner == (partner + shards_of // 2) % shards_of)
    return jnp.where(strong, factor * drawn, drawn)


def level_of(stream_key, dims, pieces, low, high):
    level, own = 1.0, jax.random.fold_in(stream_key, 6)
    for axis_at, blocks in pieces:
        heights = jnp.exp(jax.random.uniform(jax.random.fold_in(own, axis_at), (blocks,), jnp.float32, low / len(pieces), high / len(pieces)))
        level = level * jnp.repeat(heights, dims[axis_at] // blocks).reshape([-1 if axis == axis_at else 1 for axis in range(len(dims))])
    return level


def scatter_about(key, extent, width, bound, cuts=(), kind=jnp.bfloat16):
    values = jax.random.normal(key, extent, jnp.float32) * width
    if len(cuts) > 0:
        values = level_of(key, extent, cuts, -0.22, 0.18) * values
    return jnp.clip(values, min=-bound, max=bound).astype(kind)


def heavy_noise(rng, dims, width, bound, shards, heavy, kind=jnp.bfloat16):
    array = width * jax.random.normal(rng, dims, jnp.float32)
    if shards:
        array = array * level_of(rng, dims, shards, -0.22, 0.18)
    return jnp.clip(spiked(array, jax.random.fold_in(rng, 3), *heavy), -bound, bound).astype(kind)


def setup_inputs(seed: int = 0) -> dict:
    seeds = jax.random.split(jax.random.key(seed), 9)
    saved_rows = scatter_about(seeds[0], (N_DP, N_EXPERT, ROWS, D), 1.0, 6.0, ((0, 64), (1, 4), (3, 2)))
    grad_hidden = heavy_noise(seeds[1], (N_DP, N_EXPERT, HID, ROWS), 0.01, 0.15625, ((0, 64), (1, 4), (2, 2)), (0, 2, 64, 4.0))
    counts = draw_counts(jax.random.fold_in(seeds[8], 71), 0)
    offsets = draw_offsets(jax.random.fold_in(seeds[8], 71), 0)
    master = scatter_about(seeds[4], (EXPERTS, N_TENSOR, BUCKET, D), 0.2, 1.2, ((0, 4), (1, 2), (2, 64)), jnp.float32)
    moment1 = scatter_about(seeds[5], (EXPERTS, N_TENSOR, BUCKET, D), 0.5, 3.0, ((0, 4), (1, 2), (2, 64)), jnp.float32)
    moment2 = jnp.clip(jnp.exp(math.log(4.0) - 2.7725887 * jax.random.uniform(seeds[6], (EXPERTS, N_TENSOR, BUCKET, D), jnp.float32) ** level_of(seeds[6], (EXPERTS, N_TENSOR, BUCKET, D), ((0, 4), (1, 2), (2, 64)), -0.2, 0.2)), 0.25, 4.0)
    next_rows = scatter_about(seeds[7], (N_DP, EXPERTS, NEXT, D), 1.0, 6.0, ((0, 64), (1, 4), (3, 2)))
    return {"saved_rows": saved_rows, "grad_hidden": grad_hidden, "counts": counts, "offsets": offsets, "master": master, "moment1": moment1, "moment2": moment2, "next_rows": next_rows}


first_decay = 0.9
second_decay = 0.95
first_fix = 1.0 - 0.9 ** 11
second_fix = 1.0 - 0.95 ** 11
learn_rate = 0.01
weight_decay = 0.1
adam_epsilon = 1e-08

def reference(saved_rows, grad_hidden, counts, offsets, master, moment1, moment2, next_rows):
    line = jnp.arange(ROWS, dtype=jnp.int32)
    grads = []
    for expert_id in range(EXPERTS):
        group = expert_id // EXP_DEV
        begin = offsets[:, expert_id][:, None]
        finish = (offsets[:, expert_id] + counts[:, expert_id])[:, None]
        inside = ((line[None, :] >= begin) & (line[None, :] < finish)).astype(jnp.bfloat16)
        masked = grad_hidden[:, group] * inside[:, None, :]
        left = jnp.transpose(masked, (1, 0, 2)).reshape(HID, N_DP * ROWS)
        right = saved_rows[:, group].reshape(N_DP * ROWS, D)
        grads.append(jnp.dot(left, right, preferred_element_type=jnp.float32))
    grad = jnp.stack(grads).reshape(EXPERTS, N_TENSOR, BUCKET, D)
    new_moment1 = first_decay * moment1 + (1.0 - first_decay) * grad
    new_moment2 = second_decay * moment2 + (1.0 - second_decay) * grad * grad
    update = new_moment1 / first_fix / (jnp.sqrt(new_moment2 / second_fix) + adam_epsilon) + weight_decay * master
    new_master = master - learn_rate * update
    weights = new_master.astype(jnp.bfloat16).reshape(EXPERTS, HID, D)
    scale = D ** (-0.5)
    gates = []
    for expert_id in range(EXPERTS):
        inputs = next_rows[:, expert_id].reshape(N_DP * NEXT, D)
        product = jnp.dot(inputs, weights[expert_id].T, preferred_element_type=jnp.float32) * scale
        gates.append(jnp.transpose(product.reshape(N_DP, NEXT, HID), (0, 2, 1)))
    next_gate = jnp.stack(gates, axis=1)
    return (new_master, new_moment1, new_moment2, next_gate)
```

```python
import jax
import jax.numpy as jnp
from jax import lax
from jax.experimental import pallas as pl
from jax.experimental.pallas import tpu as pltpu
from jax.sharding import Mesh
from jax.sharding import PartitionSpec as P

first_decay = 0.9
second_decay = 0.95
first_fix = 1.0 - 0.9**11
second_fix = 1.0 - 0.95**11
learn_rate = 0.01
weight_decay = 0.1
adam_epsilon = 1e-08

DP = ("x", "h", "z1", "z0")
NEAR = ("x", "z0")
FAR = ("tensor", "h", "z1")
LANES = 128
COLS = 24
BLOCK = 512

VMEM = pl.BlockSpec(memory_space=pltpu.VMEM)
SMEM = pl.BlockSpec(memory_space=pltpu.SMEM)
PARAMS = pltpu.CompilerParams(vmem_limit_bytes=16 * 1024 * 1024)


def adamw(grad, weight, first, second):
    new_first = first_decay * first + (1.0 - first_decay) * grad
    new_second = second_decay * second + (1.0 - second_decay) * grad * grad
    update = (
        new_first / first_fix / (jnp.sqrt(new_second / second_fix) + adam_epsilon)
        + weight_decay * weight
    )
    return (weight - learn_rate * update, new_first, new_second)


def grad_kernel(starts, sizes, hidden, rows, out):
    i = lax.broadcasted_iota(jnp.int32, (256, 128), 0)
    c = lax.broadcasted_iota(jnp.int32, (256, 128), 1)
    z1, h, t, z0, x = (i >> 1) & 3, (i >> 3) & 1, (i >> 4) & 1, (i >> 5) & 1, i >> 6
    source = t * 64 + x * 16 + h * 8 + z1 * 2 + z0
    pick = jnp.where(c == source, 1.0, 0.0).astype(jnp.bfloat16)
    spread = jnp.dot(pick, hidden[...].reshape(128, 512), preferred_element_type=jnp.float32)
    odd = (lax.broadcasted_iota(jnp.int32, (256, 512), 0) & 1) == 1
    line = lax.broadcasted_iota(jnp.int32, (256, 512), 1)
    low = jnp.where(odd, starts[0, 1], starts[0, 0])
    high = low + jnp.where(odd, sizes[0, 1], sizes[0, 0])
    masked = jnp.where((line >= low) & (line < high), spread, 0.0).astype(jnp.bfloat16)
    for k in range(3072 // BLOCK):
        piece = jnp.dot(
            masked, rows[:, k * BLOCK : (k + 1) * BLOCK], preferred_element_type=jnp.float32
        ).astype(jnp.bfloat16)
        for j in range(BLOCK // LANES):
            out[:, k * (BLOCK // LANES) + j] = piece[:, j * LANES : (j + 1) * LANES].reshape(
                8, 32, LANES
            )


def near_sum_kernel(parts, out, total):
    for j in range(COLS):
        total[j * 32 : (j + 1) * 32] = jnp.sum(parts[:, j].astype(jnp.float32), axis=0)
    for d in range(16):
        pair = [total[pl.ds(2 * d + e, COLS, stride=32), :] for e in range(2)]
        out[d] = jnp.concatenate(pair, axis=0).astype(jnp.bfloat16)


def step_kernel(parts, master, first, second, new_master, new_first, new_second, send):
    for t in range(2):
        grad = jnp.sum(parts[t * 8 : (t + 1) * 8].astype(jnp.float32), axis=0)
        weights = []
        for e in range(2):
            at = (e, pl.ds(t * COLS, COLS), slice(None))
            results = adamw(grad[e * COLS : (e + 1) * COLS], master[at], first[at], second[at])
            new_master[at], new_first[at], new_second[at] = results
            weights.append(results[0])
        both = jnp.concatenate(weights, axis=0).astype(jnp.bfloat16)
        for d in range(8):
            send[t * 8 + d] = both


def turn_kernel(got, out, wide):
    for r in range(16):
        wide[r * 48 : (r + 1) * 48] = got[r].astype(jnp.float32)
    for k in range(48):
        block = wide[pl.ds(k, 16, stride=48), :].astype(jnp.bfloat16)
        for d in range(8):
            out[d, k] = block


def gate_kernel(weights, inputs, out):
    for e in range(2):
        total = jnp.zeros((128, 64), jnp.float32)
        for j in range(0, COLS, 2):
            left = jnp.concatenate(
                [weights[:, e * COLS + j + i].reshape(128, LANES) for i in range(2)], axis=1
            )
            total += lax.dot_general(
                left,
                inputs[e, :, j * LANES : (j + 2) * LANES],
                (((1,), (1,)), ((), ())),
                preferred_element_type=jnp.float32,
            )
        for x in range(4):
            for z0 in range(2):
                for t in range(2):
                    row = (x * 2 + z0) * 16 + t * 8
                    out[t, e, pl.ds(x * 16 + z0, 8, stride=2), :] = total[row : row + 8]


def call(kernel, out_shape, in_specs, scratch=()):
    many = isinstance(out_shape, (list, tuple))
    return pl.pallas_call(
        kernel,
        out_shape=out_shape,
        in_specs=in_specs,
        out_specs=[VMEM] * len(out_shape) if many else VMEM,
        scratch_shapes=list(scratch),
        compiler_params=PARAMS,
    )


def swap(array, axes):
    return lax.all_to_all(array, axes, 0, 0, tiled=True)


def per_device(saved_rows, grad_hidden, counts, offsets, master, moment1, moment2, next_rows):
    bf16, f32 = jnp.bfloat16, jnp.float32
    shape = jax.ShapeDtypeStruct
    hidden = swap(jnp.broadcast_to(grad_hidden[0, 0], (2, 64, 512)), "tensor")
    parts = call(grad_kernel, shape((8, COLS, 32, LANES), bf16), [SMEM, SMEM, VMEM, VMEM])(
        offsets, counts, hidden, saved_rows[0, 0]
    )
    parts = swap(parts, NEAR)
    parts = call(
        near_sum_kernel, shape((16, 48, LANES), bf16), [VMEM], [pltpu.VMEM((COLS * 32, LANES), f32)]
    )(parts)
    parts = swap(parts, FAR)
    state = [a.reshape(2, 48, LANES) for a in (master, moment1, moment2)]
    *new, send = call(
        step_kernel, [shape((2, 48, LANES), f32)] * 3 + [shape((16, 48, LANES), bf16)], [VMEM] * 4
    )(parts, *state)
    got = swap(send, FAR)
    got = call(
        turn_kernel, shape((8, 48, 16, LANES), bf16), [VMEM], [pltpu.VMEM((16 * 48, LANES), f32)]
    )(got)
    got = swap(got, NEAR)
    gates = call(gate_kernel, shape((2, 2, 64, 64), f32), [VMEM, VMEM])(got, next_rows[0])
    gates = swap(gates, "tensor")
    scale = 6144 ** (-0.5)
    next_gate = (gates[0] + gates[1]) * scale
    return (*[a.reshape(2, 1, 1, 6144) for a in new], next_gate[None])


def solution(mesh):
    fine = Mesh(
        mesh.devices.reshape(4, 2, 4, 2, 4, 2), ("x", "h", "z1", "z0", "expert", "tensor")
    )
    shard = P("expert", "tensor", DP, None)
    placed = (
        P(DP, "expert", None, "tensor"),
        P(DP, "expert", "tensor", None),
        P(DP, "expert"),
        P(DP, "expert"),
        shard,
        shard,
        shard,
        P(DP, "expert", None, "tensor"),
    )
    return jax.shard_map(
        per_device,
        mesh=fine,
        in_specs=placed,
        out_specs=(shard, shard, shard, P(DP, "expert", "tensor", None)),
        check_vma=False,
    )
```

```python
import jax
import jax.numpy as jnp
from jax import lax
from jax.experimental import pallas as pl
from jax.experimental.pallas import tpu as pltpu
from jax.sharding import Mesh
from jax.sharding import PartitionSpec as P

first_decay = 0.9
second_decay = 0.95
first_fix = 1.0 - 0.9**11
second_fix = 1.0 - 0.95**11
learn_rate = 0.01
weight_decay = 0.1
adam_epsilon = 1e-08

DP = ("x", "h", "z1", "z0")
NEAR = ("x", "z0")
FAR = ("tensor", "h", "z1")
LANES = 128
COLS = 24
BLOCK = 512
PIECES = 3072 // BLOCK
GROUP = BLOCK // LANES

VMEM = pl.BlockSpec(memory_space=pltpu.VMEM)
HBM = pl.BlockSpec(memory_space=pltpu.HBM)


def adamw(grad, weight, first, second):
    new_first = first_decay * first + (1.0 - first_decay) * grad
    new_second = second_decay * second + (1.0 - second_decay) * grad * grad
    update = (
        new_first / first_fix / (jnp.sqrt(new_second / second_fix) + adam_epsilon)
        + weight_decay * weight
    )
    return (weight - learn_rate * update, new_first, new_second)


def stage_kernel(starts, sizes, mine, rows, held, hidden, inside, start_at, size_of, sems):
    small = [
        pltpu.make_async_copy(starts, start_at, sems.at[0]),
        pltpu.make_async_copy(sizes, size_of, sems.at[1]),
    ]
    large = [
        pltpu.make_async_copy(mine, hidden, sems.at[2]),
        pltpu.make_async_copy(rows, held, sems.at[3]),
    ]
    for copy in small + large:
        copy.start()
    for copy in small:
        copy.wait()
    odd = (lax.broadcasted_iota(jnp.int32, (256, 512), 0) & 1) == 1
    line = lax.broadcasted_iota(jnp.int32, (256, 512), 1)
    low = jnp.where(odd, start_at[0, 1], start_at[0, 0])
    high = low + jnp.where(odd, size_of[0, 1], size_of[0, 0])
    inside[...] = jnp.where((line >= low) & (line < high), 1.0, 0.0).astype(jnp.bfloat16)
    for copy in large:
        copy.wait()


def grad_kernel(mine, other, inside, rows, out, ready, sems):
    stores = [
        pltpu.make_async_copy(ready.at[k], out.at[:, pl.ds(k * GROUP, GROUP)], sems.at[k])
        for k in range(PIECES)
    ]
    me = lax.axis_index("tensor")
    i = lax.broadcasted_iota(jnp.int32, (256, 64), 0)
    c = lax.broadcasted_iota(jnp.int32, (256, 64), 1)
    z1, h, t, z0, x = (i >> 1) & 3, (i >> 3) & 1, (i >> 4) & 1, (i >> 5) & 1, i >> 6
    found = c == x * 16 + h * 8 + z1 * 2 + z0
    picks = [jnp.where(found & (t == w), 1.0, 0.0).astype(jnp.bfloat16) for w in (me, 1 - me)]
    spread = jnp.dot(picks[0], mine[...], preferred_element_type=jnp.float32)
    spread += jnp.dot(picks[1], other[...], preferred_element_type=jnp.float32)
    masked = jnp.where(inside[...] != 0, spread.astype(jnp.bfloat16), 0)
    for k in range(PIECES):
        piece = jnp.dot(
            masked, rows[:, k * BLOCK : (k + 1) * BLOCK], preferred_element_type=jnp.float32
        ).astype(jnp.bfloat16)
        for j in range(GROUP):
            ready[k, :, j] = piece[:, j * LANES : (j + 1) * LANES].reshape(8, 32, LANES)
        stores[k].start()
    for copy in stores:
        copy.wait()


def near_sum_kernel(parts, unused, out, total):
    del unused
    for j in range(COLS):
        total[j * 32 : (j + 1) * 32] = jnp.sum(parts[:, j].astype(jnp.float32), axis=0)
    for d in range(16):
        pair = [total[pl.ds(2 * d + e, COLS, stride=32), :] for e in range(2)]
        out[d] = jnp.concatenate(pair, axis=0).astype(jnp.bfloat16)


def step_kernel(parts, master, first, second, new_master, new_first, new_second, send):
    weights = [[None, None], [None, None]]
    for t in range(2):
        grad = jnp.sum(parts[t * 8 : (t + 1) * 8].astype(jnp.float32), axis=0)
        for e in range(2):
            at = (e, pl.ds(t * COLS, COLS), slice(None))
            results = adamw(grad[e * COLS : (e + 1) * COLS], master[at], first[at], second[at])
            new_master[at], new_first[at], new_second[at] = results
            weights[e][t] = results[0]
    block = jnp.concatenate(weights[0] + weights[1], axis=0).astype(jnp.bfloat16)
    for d in range(8):
        send[d] = block


def turn_kernel(got, out, wide):
    for r in range(8):
        wide[r * 96 : (r + 1) * 96] = got[r].astype(jnp.float32)
    for k in range(48):
        pair = [wide[pl.ds(e * 48 + k, 8, stride=96), :] for e in range(2)]
        block = jnp.concatenate(pair, axis=0).astype(jnp.bfloat16)
        for d in range(8):
            out[d, k] = block


def gate_kernel(weights, near, far, out):
    me = lax.axis_index("tensor")
    total = jnp.zeros((128, 128), jnp.float32)
    for inputs, half in ((near, me), (far, 1 - me)):
        for j in range(0, COLS, 2):
            left = [weights[:, half * COLS + j + i].reshape(128, LANES) for i in range(2)]
            right = inputs[:, :, j * LANES : (j + 2) * LANES].reshape(128, 2 * LANES)
            total += lax.dot_general(
                jnp.concatenate(left, axis=1),
                right,
                (((1,), (1,)), ((), ())),
                preferred_element_type=jnp.float32,
            )
    total = total * (6144 ** (-0.5))
    for e in range(2):
        own = total[:, e * 64 : (e + 1) * 64]
        for x in range(4):
            for z0 in range(2):
                row = (x * 2 + z0) * 16 + e * 8
                out[e, pl.ds(x * 16 + z0, 8, stride=2), :] = own[row : row + 8]


def call(kernel, out_shape, in_specs, scratch=(), out_specs=None):
    many = isinstance(out_shape, (list, tuple))
    return pl.pallas_call(
        kernel,
        out_shape=out_shape,
        in_specs=in_specs,
        out_specs=out_specs or ([VMEM] * len(out_shape) if many else VMEM),
        scratch_shapes=list(scratch),
        compiler_params=pltpu.CompilerParams(vmem_limit_bytes=16 << 20),
    )


def swap(array, axes):
    return lax.all_to_all(array, axes, 0, 0, tiled=True)


def per_device(saved_rows, grad_hidden, counts, offsets, master, moment1, moment2, next_rows):
    bf16, f32 = jnp.bfloat16, jnp.float32
    shape = jax.ShapeDtypeStruct
    mine = grad_hidden[0, 0]
    other = lax.ppermute(mine, "tensor", [(0, 1), (1, 0)])
    far_inputs = lax.ppermute(next_rows[0], "tensor", [(0, 1), (1, 0)])
    held, hidden, inside = call(
        stage_kernel,
        [
            pltpu.VMEM((512, 3072), bf16),
            pltpu.VMEM((64, 512), bf16),
            pltpu.VMEM((256, 512), bf16),
        ],
        [HBM] * 4,
        [pltpu.SMEM((1, 2), jnp.int32)] * 2 + [pltpu.SemaphoreType.DMA((4,))],
    )(
        *[
            pltpu.with_memory_space_constraint(a, pltpu.HBM)
            for a in (offsets, counts, mine, saved_rows[0, 0])
        ]
    )
    parts = call(
        grad_kernel,
        pltpu.HBM((8, COLS, 32, LANES), bf16),
        [VMEM] * 4,
        [
            pltpu.VMEM((PIECES, 8, GROUP, 32, LANES), bf16),
            pltpu.SemaphoreType.DMA((PIECES,)),
        ],
        out_specs=HBM,
    )(hidden, other, inside, held)
    parts = swap(parts, NEAR)
    parts = call(
        near_sum_kernel,
        shape((16, 48, LANES), bf16),
        [VMEM, HBM],
        [pltpu.VMEM((COLS * 32, LANES), f32)],
    )(parts, far_inputs)
    parts = swap(parts, FAR)
    state = [a.reshape(2, 48, LANES) for a in (master, moment1, moment2)]
    *new, send = call(
        step_kernel, [shape((2, 48, LANES), f32)] * 3 + [shape((8, 96, LANES), bf16)], [VMEM] * 4
    )(parts, *state)
    got = swap(send, ("h", "z1"))
    got = call(
        turn_kernel, shape((8, 48, 16, LANES), bf16), [VMEM], [pltpu.VMEM((8 * 96, LANES), f32)]
    )(got)
    got = swap(got, NEAR)
    gates = call(gate_kernel, shape((2, 64, 64), f32), [VMEM] * 3)(
        got, next_rows[0], far_inputs
    )
    return (*[a.reshape(2, 1, 1, 6144) for a in new], gates[None])


def solution(mesh):
    fine = Mesh(
        mesh.devices.reshape(4, 2, 4, 2, 4, 2), ("x", "h", "z1", "z0", "expert", "tensor")
    )
    shard = P("expert", "tensor", DP, None)
    placed = (
        P(DP, "expert", None, "tensor"),
        P(DP, "expert", "tensor", None),
        P(DP, "expert"),
        P(DP, "expert"),
        shard,
        shard,
        shard,
        P(DP, "expert", None, "tensor"),
    )
    return jax.shard_map(
        per_device,
        mesh=fine,
        in_specs=placed,
        out_specs=(shard, shard, shard, P(DP, "expert", "tensor", None)),
        check_vma=False,
    )
```

```python
import jax
import jax.numpy as jnp
from jax import lax
from jax.experimental import pallas as pl
from jax.experimental.pallas import tpu as pltpu
from jax.sharding import Mesh
from jax.sharding import PartitionSpec as P

first_decay = 0.9
second_decay = 0.95
first_fix = 1.0 - 0.9**11
second_fix = 1.0 - 0.95**11
learn_rate = 0.01
weight_decay = 0.1
adam_epsilon = 1e-08

DP = ("x", "h", "z1", "z0")
NEAR = ("x", "z0")
FAR = ("tensor", "h", "z1")
LANES = 128
COLS = 24
BLOCK = 512
PIECES = 3072 // BLOCK
GROUP = BLOCK // LANES

VMEM = pl.BlockSpec(memory_space=pltpu.VMEM)
HBM = pl.BlockSpec(memory_space=pltpu.HBM)


def adamw(grad, weight, first, second):
    new_first = first_decay * first + (1.0 - first_decay) * grad
    new_second = second_decay * second + (1.0 - second_decay) * grad * grad
    update = (
        new_first / first_fix / (jnp.sqrt(new_second / second_fix) + adam_epsilon)
        + weight_decay * weight
    )
    return (weight - learn_rate * update, new_first, new_second)


def stage_kernel(starts, sizes, mine, rows, held, hidden, inside, start_at, size_of, sems):
    small = [
        pltpu.make_async_copy(starts, start_at, sems.at[0]),
        pltpu.make_async_copy(sizes, size_of, sems.at[1]),
    ]
    large = [
        pltpu.make_async_copy(mine, hidden, sems.at[2]),
        pltpu.make_async_copy(rows, held, sems.at[3]),
    ]
    for copy in small + large:
        copy.start()
    for copy in small:
        copy.wait()
    odd = (lax.broadcasted_iota(jnp.int32, (256, 512), 0) & 1) == 1
    line = lax.broadcasted_iota(jnp.int32, (256, 512), 1)
    low = jnp.where(odd, start_at[0, 1], start_at[0, 0])
    high = low + jnp.where(odd, size_of[0, 1], size_of[0, 0])
    inside[...] = jnp.where((line >= low) & (line < high), 1.0, 0.0).astype(jnp.bfloat16)
    for copy in large:
        copy.wait()


def grad_kernel(mine, other, inside, rows, out, ready, sems):
    stores = [
        pltpu.make_async_copy(ready.at[k], out.at[:, pl.ds(k * GROUP, GROUP)], sems.at[k])
        for k in range(PIECES)
    ]
    me = lax.axis_index("tensor")
    i = lax.broadcasted_iota(jnp.int32, (256, 64), 0)
    c = lax.broadcasted_iota(jnp.int32, (256, 64), 1)
    z1, h, t, z0, x = (i >> 1) & 3, (i >> 3) & 1, (i >> 4) & 1, (i >> 5) & 1, i >> 6
    found = c == x * 16 + h * 8 + z1 * 2 + z0
    picks = [jnp.where(found & (t == w), 1.0, 0.0).astype(jnp.bfloat16) for w in (me, 1 - me)]
    spread = jnp.dot(picks[0], mine[...], preferred_element_type=jnp.float32)
    spread += jnp.dot(picks[1], other[...], preferred_element_type=jnp.float32)
    masked = jnp.where(inside[...] != 0, spread.astype(jnp.bfloat16), 0)
    for k in range(PIECES):
        piece = jnp.dot(
            masked, rows[:, k * BLOCK : (k + 1) * BLOCK], preferred_element_type=jnp.float32
        ).astype(jnp.bfloat16)
        for j in range(GROUP):
            ready[k, :, j] = piece[:, j * LANES : (j + 1) * LANES].reshape(8, 32, LANES)
        stores[k].start()
    for copy in stores:
        copy.wait()


def near_sum_kernel(parts, out, total):
    for j in range(COLS):
        total[j * 32 : (j + 1) * 32] = jnp.sum(parts[:, j].astype(jnp.float32), axis=0)
    for d in range(16):
        pair = [total[pl.ds(2 * d + e, COLS, stride=32), :] for e in range(2)]
        out[d] = jnp.concatenate(pair, axis=0).astype(jnp.bfloat16)


def step_kernel(parts, master, first, second, new_master, new_first, new_second, send, block, sems):
    copies = [
        pltpu.make_async_copy(
            block.at[pl.ds(t * 16, 16)], send.at[pl.ds(t * 16, 16)], sems.at[t]
        )
        for t in range(2)
    ]
    for t in range(2):
        grad = jnp.sum(parts[t * 8 : (t + 1) * 8].astype(jnp.float32), axis=0)
        weights = []
        for e in range(2):
            at = (e, pl.ds(t * COLS, COLS), slice(None))
            results = adamw(grad[e * COLS : (e + 1) * COLS], master[at], first[at], second[at])
            new_master[at], new_first[at], new_second[at] = results
            weights.append(results[0])
        both = jnp.concatenate(weights, axis=0).astype(jnp.bfloat16)
        for d in range(16):
            block[t * 16 + d] = both
        copies[t].start()
    for copy in copies:
        copy.wait()


def gate_kernel(got, own, ahead, opposite, back, out, wide):
    me = lax.axis_index("x")
    step = 1 - 2 * lax.axis_index("tensor")
    for r in range(32):
        wide[r * 48 : (r + 1) * 48] = got[r].astype(jnp.float32)
    totals = []
    for e in range(2):
        total = jnp.zeros((32, 256), jnp.float32)
        for j in range(0, COLS, 2):
            left = [wide[pl.ds(e * COLS + j + i, 32, stride=48), :] for i in range(2)]
            at = (e, slice(None), pl.ds(j * LANES, 2 * LANES))
            right = [r[at] for r in (own, ahead, opposite, back)]
            total += lax.dot_general(
                jnp.concatenate(left, axis=1).astype(jnp.bfloat16),
                jnp.concatenate(right, axis=0),
                (((1,), (1,)), ((), ())),
                preferred_element_type=jnp.float32,
            )
        totals.append(total)
    for k in range(4):
        x = lax.rem(me + 4 - k * step, 4)
        for t in range(2):
            pair = [w[t * 16 : (t + 1) * 16, k * 64 : (k + 1) * 64] for w in totals]
            out[x * 2 + t] = jnp.concatenate(pair, axis=1)


def end_kernel(parts, out):
    scale = 6144 ** (-0.5)
    for x in range(4):
        total = (parts[2 * x] + parts[2 * x + 1]) * scale
        for e in range(2):
            out[e, x * 16 : (x + 1) * 16, :] = total[:, e * 64 : (e + 1) * 64]


def call(kernel, out_shape, in_specs, scratch=(), out_specs=None):
    many = isinstance(out_shape, (list, tuple))
    return pl.pallas_call(
        kernel,
        out_shape=out_shape,
        in_specs=in_specs,
        out_specs=out_specs or ([VMEM] * len(out_shape) if many else VMEM),
        scratch_shapes=list(scratch),
        compiler_params=pltpu.CompilerParams(vmem_limit_bytes=16 << 20),
    )


def shift(array, by):
    pairs = [
        (x * 2 + t, (x + (by if t == 0 else -by)) % 4 * 2 + t) for x in range(4) for t in range(2)
    ]
    return lax.ppermute(array, ("x", "tensor"), pairs)


def swap(array, axes):
    return lax.all_to_all(array, axes, 0, 0, tiled=True)


def per_device(saved_rows, grad_hidden, counts, offsets, master, moment1, moment2, next_rows):
    bf16, f32 = jnp.bfloat16, jnp.float32
    shape = jax.ShapeDtypeStruct
    mine = grad_hidden[0, 0]
    other = lax.ppermute(mine, "tensor", [(0, 1), (1, 0)])
    held, hidden, inside = call(
        stage_kernel,
        [
            pltpu.VMEM((512, 3072), bf16),
            pltpu.VMEM((64, 512), bf16),
            pltpu.VMEM((256, 512), bf16),
        ],
        [HBM] * 4,
        [pltpu.SMEM((1, 2), jnp.int32)] * 2 + [pltpu.SemaphoreType.DMA((4,))],
    )(
        *[
            pltpu.with_memory_space_constraint(a, pltpu.HBM)
            for a in (offsets, counts, mine, saved_rows[0, 0])
        ]
    )
    parts = call(
        grad_kernel,
        pltpu.HBM((8, COLS, 32, LANES), bf16),
        [VMEM] * 4,
        [
            pltpu.VMEM((PIECES, 8, GROUP, 32, LANES), bf16),
            pltpu.SemaphoreType.DMA((PIECES,)),
        ],
        out_specs=HBM,
    )(hidden, other, inside, held)
    parts = swap(parts, NEAR)
    parts, inputs = lax.optimization_barrier((parts, next_rows[0]))
    ahead, back = shift(inputs, 1), shift(inputs, -1)
    opposite = shift(ahead, 1)
    parts = call(
        near_sum_kernel,
        shape((16, 48, LANES), bf16),
        [VMEM],
        [pltpu.VMEM((COLS * 32, LANES), f32)],
    )(parts)
    parts = swap(parts, FAR)
    state = [a.reshape(2, 48, LANES) for a in (master, moment1, moment2)]
    *new, send = call(
        step_kernel,
        [shape((2, 48, LANES), f32)] * 3 + [pltpu.HBM((32, 48, LANES), bf16)],
        [VMEM] * 4,
        [pltpu.VMEM((32, 48, LANES), bf16), pltpu.SemaphoreType.DMA((2,))],
        out_specs=[VMEM] * 3 + [HBM],
    )(parts, *state)
    got = swap(send, ("tensor", "h", "z1", "z0"))
    gates = call(
        gate_kernel, shape((8, 16, LANES), f32), [VMEM] * 5, [pltpu.VMEM((32 * 48, LANES), f32)]
    )(got, inputs, ahead, opposite, back)
    gates = swap(gates, ("x", "tensor"))
    gates = call(end_kernel, shape((2, 64, 64), f32), [VMEM])(gates)
    return (*[a.reshape(2, 1, 1, 6144) for a in new], gates[None])


def solution(mesh):
    fine = Mesh(
        mesh.devices.reshape(4, 2, 4, 2, 4, 2), ("x", "h", "z1", "z0", "expert", "tensor")
    )
    shard = P("expert", "tensor", DP, None)
    placed = (
        P(DP, "expert", None, "tensor"),
        P(DP, "expert", "tensor", None),
        P(DP, "expert"),
        P(DP, "expert"),
        shard,
        shard,
        shard,
        P(DP, "expert", None, "tensor"),
    )
    return jax.shard_map(
        per_device,
        mesh=fine,
        in_specs=placed,
        out_specs=(shard, shard, shard, P(DP, "expert", "tensor", None)),
        check_vma=False,
    )
```

```python
import jax
import jax.numpy as jnp
from jax import lax
from jax.experimental import pallas as pl
from jax.experimental.pallas import tpu as pltpu
from jax.sharding import Mesh
from jax.sharding import PartitionSpec as P

first_decay = 0.9
second_decay = 0.95
first_fix = 1.0 - 0.9**11
second_fix = 1.0 - 0.95**11
learn_rate = 0.01
weight_decay = 0.1
adam_epsilon = 1e-08

DP = ("x", "h", "z1", "z0")
NEAR = ("x", "z0")
FAR = ("tensor", "h", "z1")
LANES = 128
COLS = 24
BLOCK = 512
PIECES = 3072 // BLOCK
GROUP = BLOCK // LANES
LATE = 3_000_000_000
LATER = 3_000_000_000

VMEM = pl.BlockSpec(memory_space=pltpu.VMEM)
HBM = pl.BlockSpec(memory_space=pltpu.HBM)


def adamw(grad, weight, first, second):
    new_first = first_decay * first + (1.0 - first_decay) * grad
    new_second = second_decay * second + (1.0 - second_decay) * grad * grad
    update = (
        new_first / first_fix / (jnp.sqrt(new_second / second_fix) + adam_epsilon)
        + weight_decay * weight
    )
    return (weight - learn_rate * update, new_first, new_second)


def stage_kernel(starts, sizes, mine, rows, held, hidden, inside, start_at, size_of, sems):
    small = [
        pltpu.make_async_copy(starts, start_at, sems.at[0]),
        pltpu.make_async_copy(sizes, size_of, sems.at[1]),
    ]
    large = [
        pltpu.make_async_copy(mine, hidden, sems.at[2]),
        pltpu.make_async_copy(rows, held, sems.at[3]),
    ]
    for copy in small + large:
        copy.start()
    for copy in small:
        copy.wait()
    odd = (lax.broadcasted_iota(jnp.int32, (256, 512), 0) & 1) == 1
    line = lax.broadcasted_iota(jnp.int32, (256, 512), 1)
    low = jnp.where(odd, start_at[0, 1], start_at[0, 0])
    high = low + jnp.where(odd, size_of[0, 1], size_of[0, 0])
    inside[...] = jnp.where((line >= low) & (line < high), 1.0, 0.0).astype(jnp.bfloat16)
    for copy in large:
        copy.wait()


def grad_kernel(mine, other, inside, rows, out):
    me = lax.axis_index("tensor")
    i = lax.broadcasted_iota(jnp.int32, (256, 64), 0)
    c = lax.broadcasted_iota(jnp.int32, (256, 64), 1)
    z1, h, t, z0, x = (i >> 1) & 3, (i >> 3) & 1, (i >> 4) & 1, (i >> 5) & 1, i >> 6
    found = c == x * 16 + h * 8 + z1 * 2 + z0
    picks = [jnp.where(found & (t == w), 1.0, 0.0).astype(jnp.bfloat16) for w in (me, 1 - me)]
    spread = jnp.dot(picks[0], mine[...], preferred_element_type=jnp.float32)
    spread += jnp.dot(picks[1], other[...], preferred_element_type=jnp.float32)
    masked = jnp.where(inside[...] != 0, spread.astype(jnp.bfloat16), 0)
    for k in range(PIECES):
        piece = jnp.dot(
            masked, rows[:, k * BLOCK : (k + 1) * BLOCK], preferred_element_type=jnp.float32
        ).astype(jnp.bfloat16)
        for j in range(GROUP):
            block = piece[:, j * LANES : (j + 1) * LANES]
            out[:, k * GROUP + j] = block.reshape(8, 32, LANES)


def near_sum_kernel(parts, out, total, ready, sems):
    copies = [
        pltpu.make_async_copy(ready.at[pl.ds(k * 4, 4)], out.at[pl.ds(k * 4, 4)], sems.at[k])
        for k in range(4)
    ]
    for j in range(COLS):
        total[j * 32 : (j + 1) * 32] = jnp.sum(parts[:, j].astype(jnp.float32), axis=0)
    for k in range(4):
        for d in range(4 * k, 4 * k + 4):
            pair = [total[pl.ds(2 * d + e, COLS, stride=32), :] for e in range(2)]
            ready[d] = jnp.concatenate(pair, axis=0).astype(jnp.bfloat16)
        copies[k].start()
    for copy in copies:
        copy.wait()


def step_kernel(parts, master, first, second, new_master, new_first, new_second, send, block, sems):
    copies = [
        pltpu.make_async_copy(
            block.at[pl.ds(t * 16, 16)], send.at[pl.ds(t * 16, 16)], sems.at[t]
        )
        for t in range(2)
    ]
    for t in range(2):
        grad = jnp.sum(parts[t * 8 : (t + 1) * 8].astype(jnp.float32), axis=0)
        weights = []
        for e in range(2):
            at = (e, pl.ds(t * COLS, COLS), slice(None))
            results = adamw(grad[e * COLS : (e + 1) * COLS], master[at], first[at], second[at])
            new_master[at], new_first[at], new_second[at] = results
            weights.append(results[0])
        both = jnp.concatenate(weights, axis=0).astype(jnp.bfloat16)
        for d in range(16):
            block[t * 16 + d] = both
        copies[t].start()
    for copy in copies:
        copy.wait()


def turn_kernel(got, unused, out, wide):
    del unused
    for r in range(32):
        wide[r * 48 : (r + 1) * 48] = got[r].astype(jnp.float32)
    for k in range(48):
        out[k] = wide[pl.ds(k, 32, stride=48), :].astype(jnp.bfloat16)


def gate_kernel(weights, own, ahead, opposite, back, out):
    me = lax.axis_index("x")
    step = 1 - 2 * lax.axis_index("tensor")
    inputs = (own, ahead, opposite, back)
    totals = []
    for e in range(2):
        total = jnp.zeros((32, 256), jnp.float32)
        for j in range(0, COLS, 2):
            left = [weights[e * COLS + j + i] for i in range(2)]
            at = (e, slice(None), pl.ds(j * LANES, 2 * LANES))
            right = [r[at] for r in inputs]
            total += lax.dot_general(
                jnp.concatenate(left, axis=1),
                jnp.concatenate(right, axis=0),
                (((1,), (1,)), ((), ())),
                preferred_element_type=jnp.float32,
            )
        totals.append(total)
    for k in range(4):
        x = lax.rem(me + 4 - k * step, 4)
        for t in range(2):
            pair = [w[t * 16 : (t + 1) * 16, k * 64 : (k + 1) * 64] for w in totals]
            out[x * 2 + t] = jnp.concatenate(pair, axis=1)


def end_kernel(parts, out):
    scale = 6144 ** (-0.5)
    for x in range(4):
        total = (parts[2 * x] + parts[2 * x + 1]) * scale
        for e in range(2):
            out[e, x * 16 : (x + 1) * 16, :] = total[:, e * 64 : (e + 1) * 64]


def call(kernel, out_shape, in_specs, scratch=(), out_specs=None, flops=None):
    many = isinstance(out_shape, (list, tuple))
    return pl.pallas_call(
        kernel,
        out_shape=out_shape,
        in_specs=in_specs,
        out_specs=out_specs or ([VMEM] * len(out_shape) if many else VMEM),
        scratch_shapes=list(scratch),
        cost_estimate=flops
        and pl.CostEstimate(flops=flops, bytes_accessed=0, transcendentals=0),
        compiler_params=pltpu.CompilerParams(vmem_limit_bytes=16 << 20),
    )


def shift(array, by):
    pairs = [
        (x * 2 + t, (x + (by if t == 0 else -by)) % 4 * 2 + t) for x in range(4) for t in range(2)
    ]
    return lax.ppermute(array, ("x", "tensor"), pairs)


def swap(array, axes):
    return lax.all_to_all(array, axes, 0, 0, tiled=True)


def per_device(saved_rows, grad_hidden, counts, offsets, master, moment1, moment2, next_rows):
    bf16, f32 = jnp.bfloat16, jnp.float32
    shape = jax.ShapeDtypeStruct
    mine = grad_hidden[0, 0]
    other = lax.ppermute(mine, "tensor", [(0, 1), (1, 0)])
    held, hidden, inside = call(
        stage_kernel,
        [
            pltpu.VMEM((512, 3072), bf16),
            pltpu.VMEM((64, 512), bf16),
            pltpu.VMEM((256, 512), bf16),
        ],
        [HBM] * 4,
        [pltpu.SMEM((1, 2), jnp.int32)] * 2 + [pltpu.SemaphoreType.DMA((4,))],
    )(
        *[
            pltpu.with_memory_space_constraint(a, pltpu.HBM)
            for a in (offsets, counts, mine, saved_rows[0, 0])
        ]
    )
    parts = call(
        grad_kernel,
        pltpu.VMEM((8, COLS, 32, LANES), bf16),
        [VMEM] * 4,
    )(hidden, other, inside, held)
    parts = swap(parts, NEAR)
    parts, inputs = lax.optimization_barrier((parts, next_rows[0]))
    ahead, back = shift(inputs, 1), shift(inputs, -1)
    parts = call(
        near_sum_kernel,
        pltpu.HBM((16, 48, LANES), bf16),
        [VMEM],
        [
            pltpu.VMEM((COLS * 32, LANES), f32),
            pltpu.VMEM((16, 48, LANES), bf16),
            pltpu.SemaphoreType.DMA((4,)),
        ],
        out_specs=HBM,
    )(parts)
    parts = swap(parts, FAR)
    state = [a.reshape(2, 48, LANES) for a in (master, moment1, moment2)]
    *new, send = call(
        step_kernel,
        [shape((2, 48, LANES), f32)] * 3 + [pltpu.HBM((32, 48, LANES), bf16)],
        [VMEM] * 4,
        [pltpu.VMEM((32, 48, LANES), bf16), pltpu.SemaphoreType.DMA((2,))],
        out_specs=[VMEM] * 3 + [HBM],
        flops=LATE,
    )(parts, *state)
    got = swap(send, ("tensor", "h", "z1", "z0"))
    relayed, new[0] = lax.optimization_barrier((ahead, new[0]))
    opposite = shift(relayed, 1)
    weights = call(
        turn_kernel,
        shape((48, 32, LANES), bf16),
        [VMEM, HBM],
        [pltpu.VMEM((32 * 48, LANES), f32)],
        flops=LATER,
    )(got, back)
    gates = call(gate_kernel, shape((8, 16, LANES), f32), [VMEM] * 5)(
        weights, inputs, ahead, opposite, back
    )
    gates = swap(gates, ("x", "tensor"))
    gates = call(end_kernel, shape((2, 64, 64), f32), [VMEM])(gates)
    return (*[a.reshape(2, 1, 1, 6144) for a in new], gates[None])


def solution(mesh):
    fine = Mesh(
        mesh.devices.reshape(4, 2, 4, 2, 4, 2), ("x", "h", "z1", "z0", "expert", "tensor")
    )
    shard = P("expert", "tensor", DP, None)
    placed = (
        P(DP, "expert", None, "tensor"),
        P(DP, "expert", "tensor", None),
        P(DP, "expert"),
        P(DP, "expert"),
        shard,
        shard,
        shard,
        P(DP, "expert", None, "tensor"),
    )
    return jax.shard_map(
        per_device,
        mesh=fine,
        in_specs=placed,
        out_specs=(shard, shard, shard, P(DP, "expert", "tensor", None)),
        check_vma=False,
    )
```

```python
import jax
import jax.numpy as jnp
from jax import lax
from jax.experimental import pallas as pl
from jax.experimental.pallas import tpu as pltpu
from jax.sharding import Mesh
from jax.sharding import PartitionSpec as P

first_decay = 0.9
second_decay = 0.95
first_fix = 1.0 - 0.9**11
second_fix = 1.0 - 0.95**11
learn_rate = 0.01
weight_decay = 0.1
adam_epsilon = 1e-08

DP = ("x1", "x0", "h", "z1", "z0")
PLANE = ("x1", "x0", "z1", "z0", "tensor")
FAR = ("tensor", "x1", "h", "z1")
LANES = 128
COLS = 24
BLOCK = 512
PIECES = 3072 // BLOCK
GROUP = BLOCK // LANES
LATE = 3_000_000_000
LATER = 3_000_000_000

VMEM = pl.BlockSpec(memory_space=pltpu.VMEM)
HBM = pl.BlockSpec(memory_space=pltpu.HBM)


def adamw(grad, weight, first, second):
    new_first = first_decay * first + (1.0 - first_decay) * grad
    new_second = second_decay * second + (1.0 - second_decay) * grad * grad
    update = (
        new_first / first_fix / (jnp.sqrt(new_second / second_fix) + adam_epsilon)
        + weight_decay * weight
    )
    return (weight - learn_rate * update, new_first, new_second)


def stage_kernel(starts, sizes, mine, rows, held, hidden, inside, start_at, size_of, sems):
    small = [
        pltpu.make_async_copy(starts, start_at, sems.at[0]),
        pltpu.make_async_copy(sizes, size_of, sems.at[1]),
    ]
    large = [
        pltpu.make_async_copy(mine, hidden, sems.at[2]),
        pltpu.make_async_copy(rows, held, sems.at[3]),
    ]
    for copy in small + large:
        copy.start()
    for copy in small:
        copy.wait()
    odd = (lax.broadcasted_iota(jnp.int32, (256, 512), 0) & 1) == 1
    line = lax.broadcasted_iota(jnp.int32, (256, 512), 1)
    low = jnp.where(odd, start_at[0, 1], start_at[0, 0])
    high = low + jnp.where(odd, size_of[0, 1], size_of[0, 0])
    inside[...] = jnp.where((line >= low) & (line < high), 1.0, 0.0).astype(jnp.bfloat16)
    for copy in large:
        copy.wait()


def grad_kernel(mine, other, inside, rows, out):
    me = lax.axis_index("tensor")
    i = lax.broadcasted_iota(jnp.int32, (256, 64), 0)
    c = lax.broadcasted_iota(jnp.int32, (256, 64), 1)
    z1, h, x1, t = (i >> 1) & 3, (i >> 3) & 1, (i >> 4) & 1, (i >> 5) & 1
    z0, x0 = (i >> 6) & 1, i >> 7
    found = c == x1 * 32 + x0 * 16 + h * 8 + z1 * 2 + z0
    picks = [jnp.where(found & (t == w), 1.0, 0.0).astype(jnp.bfloat16) for w in (me, 1 - me)]
    spread = jnp.dot(picks[0], mine[...], preferred_element_type=jnp.float32)
    spread += jnp.dot(picks[1], other[...], preferred_element_type=jnp.float32)
    masked = jnp.where(inside[...] != 0, spread.astype(jnp.bfloat16), 0)
    for k in range(PIECES):
        piece = jnp.dot(
            masked, rows[:, k * BLOCK : (k + 1) * BLOCK], preferred_element_type=jnp.float32
        ).astype(jnp.bfloat16)
        for j in range(GROUP):
            block = piece[:, j * LANES : (j + 1) * LANES]
            out[:, k * GROUP + j] = block.reshape(4, 64, LANES)


def near_sum_kernel(parts, out, total, ready, sems):
    copies = [
        pltpu.make_async_copy(ready.at[pl.ds(k * 8, 8)], out.at[pl.ds(k * 8, 8)], sems.at[k])
        for k in range(4)
    ]
    for j in range(COLS):
        total[j * 64 : (j + 1) * 64] = jnp.sum(parts[:, j].astype(jnp.float32), axis=0)
    for k in range(4):
        for d in range(8 * k, 8 * k + 8):
            pair = [total[pl.ds(2 * d + e, COLS, stride=64), :] for e in range(2)]
            ready[d] = jnp.concatenate(pair, axis=0).astype(jnp.bfloat16)
        copies[k].start()
    for copy in copies:
        copy.wait()


def step_kernel(parts, master, first, second, new_master, new_first, new_second, send, block, sems):
    copies = [
        pltpu.make_async_copy(
            block.at[pl.ds(t * 16, 16)], send.at[pl.ds(t * 16, 16)], sems.at[t]
        )
        for t in range(2)
    ]
    for t in range(2):
        grad = jnp.sum(parts[t * 16 : (t + 1) * 16].astype(jnp.float32), axis=0)
        weights = []
        for e in range(2):
            at = (e, pl.ds(t * COLS, COLS), slice(None))
            results = adamw(grad[e * COLS : (e + 1) * COLS], master[at], first[at], second[at])
            new_master[at], new_first[at], new_second[at] = results
            weights.append(results[0])
        both = jnp.concatenate(weights, axis=0).astype(jnp.bfloat16)
        for d in range(16):
            block[t * 16 + d] = both
        copies[t].start()
    for copy in copies:
        copy.wait()


def turn_kernel(got, unused, out, wide):
    del unused
    for r in range(32):
        wide[r * 48 : (r + 1) * 48] = got[r].astype(jnp.float32)
    for k in range(48):
        out[k] = wide[pl.ds(k, 32, stride=48), :].astype(jnp.bfloat16)


def gate_kernel(weights, own, ahead, opposite, back, out):
    me = lax.axis_index("x1") * 2 + lax.axis_index("x0")
    step = 1 - 2 * lax.axis_index("tensor")
    inputs = (own, ahead, opposite, back)
    totals = []
    for e in range(2):
        total = jnp.zeros((32, 256), jnp.float32)
        for j in range(0, COLS, 2):
            left = [weights[e * COLS + j + i] for i in range(2)]
            at = (e, slice(None), pl.ds(j * LANES, 2 * LANES))
            right = [r[at] for r in inputs]
            total += lax.dot_general(
                jnp.concatenate(left, axis=1),
                jnp.concatenate(right, axis=0),
                (((1,), (1,)), ((), ())),
                preferred_element_type=jnp.float32,
            )
        totals.append(total)
    for k in range(4):
        x = lax.rem(me + 4 - k * step, 4)
        for t in range(2):
            pair = [w[t * 16 : (t + 1) * 16, k * 64 : (k + 1) * 64] for w in totals]
            out[x * 2 + t] = jnp.concatenate(pair, axis=1)


def end_kernel(parts, out):
    scale = 6144 ** (-0.5)
    for x in range(4):
        total = (parts[2 * x] + parts[2 * x + 1]) * scale
        for e in range(2):
            out[e, x * 16 : (x + 1) * 16, :] = total[:, e * 64 : (e + 1) * 64]


def call(kernel, out_shape, in_specs, scratch=(), out_specs=None, flops=None):
    many = isinstance(out_shape, (list, tuple))
    return pl.pallas_call(
        kernel,
        out_shape=out_shape,
        in_specs=in_specs,
        out_specs=out_specs or ([VMEM] * len(out_shape) if many else VMEM),
        scratch_shapes=list(scratch),
        cost_estimate=flops
        and pl.CostEstimate(flops=flops, bytes_accessed=0, transcendentals=0),
        compiler_params=pltpu.CompilerParams(vmem_limit_bytes=16 << 20),
    )


def shift(array, by):
    pairs = [
        (x * 2 + t, (x + (by if t == 0 else -by)) % 4 * 2 + t) for x in range(4) for t in range(2)
    ]
    return lax.ppermute(array, ("x1", "x0", "tensor"), pairs)


def squares():
    found = []
    for t in range(2):
        for x in range(t, 4, 2):
            for z in range(t, 8, 2):
                xs = sorted((x, (x + 1) % 4), key=lambda i: i % 2)
                zs = sorted((z, (z + 1) % 8), key=lambda i: i % 2)
                found.append([(i * 8 + k) * 2 + t for i in xs for k in zs])
    return found


def swap(array, axes):
    return lax.all_to_all(array, axes, 0, 0, tiled=True)


def per_device(saved_rows, grad_hidden, counts, offsets, master, moment1, moment2, next_rows):
    bf16, f32 = jnp.bfloat16, jnp.float32
    shape = jax.ShapeDtypeStruct
    mine = grad_hidden[0, 0]
    other = lax.ppermute(mine, "tensor", [(0, 1), (1, 0)])
    held, hidden, inside = call(
        stage_kernel,
        [
            pltpu.VMEM((512, 3072), bf16),
            pltpu.VMEM((64, 512), bf16),
            pltpu.VMEM((256, 512), bf16),
        ],
        [HBM] * 4,
        [pltpu.SMEM((1, 2), jnp.int32)] * 2 + [pltpu.SemaphoreType.DMA((4,))],
    )(
        *[
            pltpu.with_memory_space_constraint(a, pltpu.HBM)
            for a in (offsets, counts, mine, saved_rows[0, 0])
        ]
    )
    parts = call(
        grad_kernel,
        pltpu.VMEM((4, COLS, 64, LANES), bf16),
        [VMEM] * 4,
    )(hidden, other, inside, held)
    parts = lax.all_to_all(parts, PLANE, 0, 0, tiled=True, axis_index_groups=squares())
    parts, inputs = lax.optimization_barrier((parts, next_rows[0]))
    ahead, back = shift(inputs, 1), shift(inputs, -1)
    parts = call(
        near_sum_kernel,
        pltpu.HBM((32, 48, LANES), bf16),
        [VMEM],
        [
            pltpu.VMEM((COLS * 64, LANES), f32),
            pltpu.VMEM((32, 48, LANES), bf16),
            pltpu.SemaphoreType.DMA((4,)),
        ],
        out_specs=HBM,
    )(parts)
    parts = swap(parts, FAR)
    state = [a.reshape(2, 48, LANES) for a in (master, moment1, moment2)]
    *new, send = call(
        step_kernel,
        [shape((2, 48, LANES), f32)] * 3 + [pltpu.HBM((32, 48, LANES), bf16)],
        [VMEM] * 4,
        [pltpu.VMEM((32, 48, LANES), bf16), pltpu.SemaphoreType.DMA((2,))],
        out_specs=[VMEM] * 3 + [HBM],
        flops=LATE,
    )(parts, *state)
    got = swap(send, ("tensor", "h", "z1", "z0"))
    relayed, new[0] = lax.optimization_barrier((ahead, new[0]))
    opposite = shift(relayed, 1)
    weights = call(
        turn_kernel,
        shape((48, 32, LANES), bf16),
        [VMEM, HBM],
        [pltpu.VMEM((32 * 48, LANES), f32)],
        flops=LATER,
    )(got, back)
    gates = call(gate_kernel, shape((8, 16, LANES), f32), [VMEM] * 5)(
        weights, inputs, ahead, opposite, back
    )
    gates = swap(gates, ("x1", "x0", "tensor"))
    gates = call(end_kernel, shape((2, 64, 64), f32), [VMEM])(gates)
    return (*[a.reshape(2, 1, 1, 6144) for a in new], gates[None])


def solution(mesh):
    fine = Mesh(
        mesh.devices.reshape(2, 2, 2, 4, 2, 4, 2),
        ("x1", "x0", "h", "z1", "z0", "expert", "tensor"),
    )
    shard = P("expert", "tensor", DP, None)
    placed = (
        P(DP, "expert", None, "tensor"),
        P(DP, "expert", "tensor", None),
        P(DP, "expert"),
        P(DP, "expert"),
        shard,
        shard,
        shard,
        P(DP, "expert", None, "tensor"),
    )
    return jax.shard_map(
        per_device,
        mesh=fine,
        in_specs=placed,
        out_specs=(shard, shard, shard, P(DP, "expert", "tensor", None)),
        check_vma=False,
    )
```

```python
import jax
import jax.numpy as jnp
from jax import lax
from jax.experimental import pallas as pl
from jax.experimental.pallas import tpu as pltpu
from jax.sharding import Mesh
from jax.sharding import PartitionSpec as P

first_decay = 0.9
second_decay = 0.95
first_fix = 1.0 - 0.9**11
second_fix = 1.0 - 0.95**11
learn_rate = 0.01
weight_decay = 0.1
adam_epsilon = 1e-08

DP = ("x1", "x0", "h", "z1", "z0")
PLANE = ("x1", "x0", "z1", "z0", "tensor")
FAR = ("x1", "h", "z1")
LANES = 128
COLS = 24
BLOCK = 512
PIECES = 3072 // BLOCK
GROUP = BLOCK // LANES
LATE = 3_000_000_000
LATER = 3_000_000_000

VMEM = pl.BlockSpec(memory_space=pltpu.VMEM)
HBM = pl.BlockSpec(memory_space=pltpu.HBM)


def adamw(grad, weight, first, second):
    new_first = first_decay * first + (1.0 - first_decay) * grad
    new_second = second_decay * second + (1.0 - second_decay) * grad * grad
    update = (
        new_first / first_fix / (jnp.sqrt(new_second / second_fix) + adam_epsilon)
        + weight_decay * weight
    )
    return (weight - learn_rate * update, new_first, new_second)


def stage_kernel(starts, sizes, mine, rows, held, hidden, inside, start_at, size_of, sems):
    small = [
        pltpu.make_async_copy(starts, start_at, sems.at[0]),
        pltpu.make_async_copy(sizes, size_of, sems.at[1]),
    ]
    large = [
        pltpu.make_async_copy(mine, hidden, sems.at[2]),
        pltpu.make_async_copy(rows, held, sems.at[3]),
    ]
    for copy in small + large:
        copy.start()
    for copy in small:
        copy.wait()
    odd = (lax.broadcasted_iota(jnp.int32, (256, 512), 0) & 1) == 1
    line = lax.broadcasted_iota(jnp.int32, (256, 512), 1)
    low = jnp.where(odd, start_at[0, 1], start_at[0, 0])
    high = low + jnp.where(odd, size_of[0, 1], size_of[0, 0])
    inside[...] = jnp.where((line >= low) & (line < high), 1.0, 0.0).astype(jnp.bfloat16)
    for copy in large:
        copy.wait()


def grad_kernel(mine, other, inside, rows, out):
    me = lax.axis_index("tensor")
    i = lax.broadcasted_iota(jnp.int32, (256, 64), 0)
    c = lax.broadcasted_iota(jnp.int32, (256, 64), 1)
    t, z1, h, x1 = (i >> 1) & 1, (i >> 2) & 3, (i >> 4) & 1, (i >> 5) & 1
    z0, x0 = (i >> 6) & 1, i >> 7
    found = c == x1 * 32 + x0 * 16 + h * 8 + z1 * 2 + z0
    picks = [jnp.where(found & (t == w), 1.0, 0.0).astype(jnp.bfloat16) for w in (me, 1 - me)]
    spread = jnp.dot(picks[0], mine[...], preferred_element_type=jnp.float32)
    spread += jnp.dot(picks[1], other[...], preferred_element_type=jnp.float32)
    masked = jnp.where(inside[...] != 0, spread.astype(jnp.bfloat16), 0)
    for k in range(PIECES):
        piece = jnp.dot(
            masked, rows[:, k * BLOCK : (k + 1) * BLOCK], preferred_element_type=jnp.float32
        ).astype(jnp.bfloat16)
        for j in range(GROUP):
            block = piece[:, j * LANES : (j + 1) * LANES]
            out[:, k * GROUP + j] = block.reshape(4, 64, LANES)


def near_sum_kernel(parts, out, total, ready, sems):
    copies = [
        pltpu.make_async_copy(ready.at[pl.ds(k * 4, 4)], out.at[pl.ds(k * 4, 4)], sems.at[k])
        for k in range(4)
    ]
    for j in range(COLS):
        total[j * 64 : (j + 1) * 64] = jnp.sum(parts[:, j].astype(jnp.float32), axis=0)
    for k in range(4):
        for d in range(4 * k, 4 * k + 4):
            pair = [total[pl.ds(4 * d + e, COLS, stride=64), :] for e in range(4)]
            ready[d] = jnp.concatenate(pair, axis=0).astype(jnp.bfloat16)
        copies[k].start()
    for copy in copies:
        copy.wait()


def step_kernel(parts, near, far, new_near, new_far, send, block, sem):
    me = lax.axis_index("tensor")
    half = pl.ds(pl.multiple_of(me * COLS, COLS), COLS)
    grad = jnp.sum(parts[...].astype(jnp.float32), axis=0)
    mine = []
    for state, new, t in ((near, new_near, 0), (far, new_far, 1)):
        for e in range(2):
            low, high = (grad[(w * 2 + e) * COLS : (w * 2 + e + 1) * COLS] for w in range(2))
            own = jnp.where(me == t, low, high)
            results = adamw(own, *[state[2 * i + e, half, :] for i in range(3)])
            for i in range(3):
                new[2 * i + e] = results[i]
            mine.append(results[0])
    first = [jnp.where(me == 0, mine[e], mine[2 + e]) for e in range(2)]
    second = [jnp.where(me == 0, mine[2 + e], mine[e]) for e in range(2)]
    both = jnp.concatenate(first + second, axis=0).astype(jnp.bfloat16)
    for d in range(16):
        block[d] = both
    copy = pltpu.make_async_copy(block, send, sem)
    copy.start()
    copy.wait()


def join_kernel(near, far, *out):
    me = lax.axis_index("tensor")
    for part, t in ((near, me), (far, 1 - me)):
        half = pl.ds(pl.multiple_of(t * COLS, COLS), COLS)
        for i in range(3):
            for e in range(2):
                out[i][e, half, :] = part[2 * i + e]


def turn_kernel(got, unused, out, wide):
    del unused
    for r in range(16):
        for t in range(2):
            row = t * 16 + r
            at = pl.ds(t * 48, 48)
            wide[row * 48 : (row + 1) * 48] = got[r, at, :].astype(jnp.float32)
    for k in range(48):
        out[k] = wide[pl.ds(k, 32, stride=48), :].astype(jnp.bfloat16)


def gate_kernel(weights, own, ahead, opposite, back, out):
    me = lax.axis_index("x1") * 2 + lax.axis_index("x0")
    step = 1 - 2 * lax.axis_index("tensor")
    inputs = (own, ahead, opposite, back)
    totals = []
    for e in range(2):
        total = jnp.zeros((32, 256), jnp.float32)
        for j in range(0, COLS, 2):
            left = [weights[e * COLS + j + i] for i in range(2)]
            at = (e, slice(None), pl.ds(j * LANES, 2 * LANES))
            right = [r[at] for r in inputs]
            total += lax.dot_general(
                jnp.concatenate(left, axis=1),
                jnp.concatenate(right, axis=0),
                (((1,), (1,)), ((), ())),
                preferred_element_type=jnp.float32,
            )
        totals.append(total)
    for k in range(4):
        x = lax.rem(me + 4 - k * step, 4)
        for t in range(2):
            pair = [w[t * 16 : (t + 1) * 16, k * 64 : (k + 1) * 64] for w in totals]
            out[x * 2 + t] = jnp.concatenate(pair, axis=1)


def end_kernel(parts, out):
    scale = 6144 ** (-0.5)
    for x in range(4):
        total = (parts[2 * x] + parts[2 * x + 1]) * scale
        for e in range(2):
            out[e, x * 16 : (x + 1) * 16, :] = total[:, e * 64 : (e + 1) * 64]


def call(kernel, out_shape, in_specs, scratch=(), out_specs=None, flops=None):
    many = isinstance(out_shape, (list, tuple))
    return pl.pallas_call(
        kernel,
        out_shape=out_shape,
        in_specs=in_specs,
        out_specs=out_specs or ([VMEM] * len(out_shape) if many else VMEM),
        scratch_shapes=list(scratch),
        cost_estimate=flops
        and pl.CostEstimate(flops=flops, bytes_accessed=0, transcendentals=0),
        compiler_params=pltpu.CompilerParams(vmem_limit_bytes=16 << 20),
    )


def shift(array, by):
    pairs = [
        (x * 2 + t, (x + (by if t == 0 else -by)) % 4 * 2 + t) for x in range(4) for t in range(2)
    ]
    return lax.ppermute(array, ("x1", "x0", "tensor"), pairs)


def squares():
    found = []
    for t in range(2):
        for x in range(t, 4, 2):
            for z in range(t, 8, 2):
                xs = sorted((x, (x + 1) % 4), key=lambda i: i % 2)
                zs = sorted((z, (z + 1) % 8), key=lambda i: i % 2)
                found.append([(i * 8 + k) * 2 + t for i in xs for k in zs])
    return found


def swap(array, axes):
    return lax.all_to_all(array, axes, 0, 0, tiled=True)


def per_device(saved_rows, grad_hidden, counts, offsets, master, moment1, moment2, next_rows):
    bf16, f32 = jnp.bfloat16, jnp.float32
    shape = jax.ShapeDtypeStruct
    mine = grad_hidden[0, 0]
    other = lax.ppermute(mine, "tensor", [(0, 1), (1, 0)])
    held, hidden, inside = call(
        stage_kernel,
        [
            pltpu.VMEM((512, 3072), bf16),
            pltpu.VMEM((64, 512), bf16),
            pltpu.VMEM((256, 512), bf16),
        ],
        [HBM] * 4,
        [pltpu.SMEM((1, 2), jnp.int32)] * 2 + [pltpu.SemaphoreType.DMA((4,))],
    )(
        *[
            pltpu.with_memory_space_constraint(a, pltpu.HBM)
            for a in (offsets, counts, mine, saved_rows[0, 0])
        ]
    )
    parts = call(
        grad_kernel,
        pltpu.VMEM((4, COLS, 64, LANES), bf16),
        [VMEM] * 4,
    )(hidden, other, inside, held)
    parts = lax.all_to_all(parts, PLANE, 0, 0, tiled=True, axis_index_groups=squares())
    parts, inputs = lax.optimization_barrier((parts, next_rows[0]))
    ahead, back = shift(inputs, 1), shift(inputs, -1)
    parts = call(
        near_sum_kernel,
        pltpu.HBM((16, 96, LANES), bf16),
        [VMEM],
        [
            pltpu.VMEM((COLS * 64, LANES), f32),
            pltpu.VMEM((16, 96, LANES), bf16),
            pltpu.SemaphoreType.DMA((4,)),
        ],
        out_specs=HBM,
    )(parts)
    parts = swap(parts, FAR)
    state = jnp.concatenate([a.reshape(2, 48, LANES) for a in (master, moment1, moment2)])
    flip = [(0, 1), (1, 0)]
    far_state = lax.ppermute(state, "tensor", flip)
    new_near, new_far, send = call(
        step_kernel,
        [shape((6, COLS, LANES), f32)] * 2 + [pltpu.HBM((16, 96, LANES), bf16)],
        [VMEM] * 3,
        [pltpu.VMEM((16, 96, LANES), bf16), pltpu.SemaphoreType.DMA],
        out_specs=[VMEM] * 2 + [HBM],
        flops=LATE,
    )(parts, state, far_state)
    got = swap(send, ("h", "z1", "z0"))
    relayed, new_near = lax.optimization_barrier((ahead, new_near))
    opposite = shift(relayed, 1)
    new = call(join_kernel, [shape((2, 48, LANES), f32)] * 3, [VMEM] * 2)(
        new_near, lax.ppermute(new_far, "tensor", flip)
    )
    weights = call(
        turn_kernel,
        shape((48, 32, LANES), bf16),
        [VMEM, HBM],
        [pltpu.VMEM((32 * 48, LANES), f32)],
        flops=LATER,
    )(got, back)
    gates = call(gate_kernel, shape((8, 16, LANES), f32), [VMEM] * 5)(
        weights, inputs, ahead, opposite, back
    )
    gates = swap(gates, ("x1", "x0", "tensor"))
    gates = call(end_kernel, shape((2, 64, 64), f32), [VMEM])(gates)
    return (*[a.reshape(2, 1, 1, 6144) for a in new], gates[None])


def solution(mesh):
    fine = Mesh(
        mesh.devices.reshape(2, 2, 2, 4, 2, 4, 2),
        ("x1", "x0", "h", "z1", "z0", "expert", "tensor"),
    )
    shard = P("expert", "tensor", DP, None)
    placed = (
        P(DP, "expert", None, "tensor"),
        P(DP, "expert", "tensor", None),
        P(DP, "expert"),
        P(DP, "expert"),
        shard,
        shard,
        shard,
        P(DP, "expert", None, "tensor"),
    )
    return jax.shard_map(
        per_device,
        mesh=fine,
        in_specs=placed,
        out_specs=(shard, shard, shard, P(DP, "expert", "tensor", None)),
        check_vma=False,
    )
```
